256 devices in a mesh: group: 8 (over z_hi, core), expert: 32 (over x, y, z_lo).
Axes of the slice: x: 4, y: 4, z: 8 (z_hi: 4, z_lo: 2; z = z_hi * 2 + z_lo), core: 2. Of those that a mesh axis runs over, the one named last changes fastest.
Arguments:
- dy_rows: bfloat16 [8, 32, 768, 3584], P('group', 'expert'), may hold values from -0.3125 to 0.3125
- hidden_rows: bfloat16 [8, 32, 768, 128], P('group', 'expert'), may hold values from -6 to 6
- row_counts: int32 [8, 32, 32, 2], P('group', 'expert'), may hold values from 0 to 24, as said below
- hot_owner: int32 [32], P('expert'), may hold values from 0 to 7
- master: float32 [8, 32, 128, 3584], P('group', 'expert'), may hold values from -0.5 to 0.5
- moment1: bfloat16 [8, 32, 128, 3584], P('group', 'expert'), may hold values from -1.796875 to 1.796875
- moment2: bfloat16 [8, 32, 128, 3584], P('group', 'expert'), may hold values from 0.019897461 to 0.5
Outputs:
- new_master: float32 [8, 32, 128, 3584], P('group', 'expert')
- new_moment1: bfloat16 [8, 32, 128, 3584], P('group', 'expert')
- new_moment2: bfloat16 [8, 32, 128, 3584], P('group', 'expert')
- replica_panel: bfloat16 [8, 32, 128, 3584], P('group', 'expert')
The draws below stay inside these ranges and needn't reach their ends.
Inputs may be any that keep to these rules, and one draw needn't show every extreme that they name: row_counts[g, d, s, 0] + row_counts[g, d, s, 1] <= 24; the own rows come first in each block, then the hot rows; every receiving device has a block that is full.
All inputs are finite; a program needn't handle non-finite values.
Results may differ from the reference program's by a relative error of at most 0.0012.
Values may be sent and summed in bfloat16 or wider, within the bound.
A program may use at most 128 MiB of HBM per device.

```python
import math
import jax
import jax.numpy as jnp
from jax import lax

WIN = 3584
HID = 128
CAP = 24
ROWS = 768
N_GROUP = 8
N_EXPERT = 32


def draw_row_counts(key, part):
    key = jax.random.fold_in(key, 7)
    key_total, key_own, key_full = jax.random.split(key, 3)
    shape = (N_GROUP, N_EXPERT, N_EXPERT)
    totals = jax.random.randint(key_total, shape, CAP // 2, CAP + 1)
    full_source = jax.random.randint(key_full, (N_GROUP, N_EXPERT, 1), 0, N_EXPERT)
    source_index = jnp.arange(N_EXPERT, dtype=jnp.int32)[None, None, :]
    totals = jnp.where(source_index == full_source, CAP, totals)
    own_count = jax.random.randint(key_own, shape, totals - totals // 2, totals + 1)
    hot_count = totals - own_count
    return jnp.stack([own_count, hot_count], axis=-1).astype(jnp.int32)


def with_ends(drawn, stream_key, low, high):
    extent = drawn.shape
    spot = [jax.random.randint(jax.random.fold_in(stream_key, axis), (), 0, extent[axis]) for axis in range(len(extent))]
    drawn = drawn.at[tuple(spot)].set(low)
    longest = extent.index(max(extent))
    spot[longest] = (spot[longest] + 1) % extent[longest]
    return drawn.at[tuple(spot)].set(high)


def spiked(entries, rng, source, target, shards_of, factor):
    owner, partner = [(jnp.arange(entries.shape[axis_at]) // (entries.shape[axis_at] // shards_of)).reshape([-1 if axis == axis_at else 1 for axis in range(entries.ndim)]) for axis_at in (source, target)]
    chosen = jax.random.permutation(rng, shards_of)[partner]
    strong = (owner == chosen) | (owner == (partner + shards_of // 2) % shards_of)
    return jnp.where(strong, factor * entries, entries)


def level_of(stream_key, shape, cuts, smallest, high):
    level, own = 1.0, jax.random.fold_in(stream_key, 6)
    for dim, parts in cuts:
        draws = jnp.exp(jax.random.uniform(jax.random.fold_in(own, dim), (parts,), jnp.float32, smallest / len(cuts), high / len(cuts)))
        level = level * jnp.repeat(draws, shape[dim] // parts).reshape([-1 if axis == dim else 1 for axis in range(len(shape))])
    return level


def bell_draw(rng, dims, spread, bound, cuts=(), kind=jnp.bfloat16):
    gain = level_of(rng, dims, cuts, -0.22, 0.18) if cuts else 1.0
    array = jax.random.normal(rng, dims, jnp.float32) * spread * gain
    return jnp.minimum(jnp.maximum(array, -bound), bound).astype(kind)


def heavy_noise(own_key, dims, deviation, limit, cuts, heavy, kind=jnp.bfloat16):
    entries = deviation * jax.random.normal(own_key, dims, jnp.float32)
    if cuts:
        entries = entries * level_of(own_key, dims, cuts, -0.22, 0.18)
    return jnp.clip(spiked(entries, jax.random.fold_in(own_key, 3), *heavy), -limit, limit).astype(kind)


def setup_inputs(seed: int = 0) -> dict:
    streams_of = jax.random.split(jax.random.key(seed), 8)
    dy_rows = heavy_noise(streams_of[0], (N_GROUP, N_EXPERT, ROWS, WIN), (2 * ROWS) ** -0.5, 0.3125, ((0, 8), (1, 32)), (1, 2, 32, 2.75))
    hidden_rows = bell_draw(streams_of[1], (N_GROUP, N_EXPERT, ROWS, HID), 1.0, 6.0, ((0, 8), (1, 32)))
    row_counts = draw_row_counts(jax.random.fold_in(streams_of[7], 71), 0)
    hot_owner = with_ends(jax.random.randint(streams_of[3], (N_EXPERT,), 0, N_GROUP), jax.random.fold_in(streams_of[3], 1), 0, N_GROUP - 1).astype(jnp.int32)
    master = bell_draw(streams_of[4], (N_GROUP, N_EXPERT, HID, WIN), HID ** -0.5, 0.5, ((0, 8), (1, 32)), jnp.float32)
    moment1 = bell_draw(streams_of[5], (N_GROUP, N_EXPERT, HID, WIN), 0.3, 1.796875, ((0, 8), (1, 32)))
    moment2 = jnp.clip(jnp.exp(math.log(0.5) - 3.224016 * jax.random.uniform(streams_of[6], (N_GROUP, N_EXPERT, HID, WIN), jnp.float32) ** level_of(streams_of[6], (N_GROUP, N_EXPERT, HID, WIN), ((0, 8), (1, 32)), -0.2, 0.2)), 0.019897461, 0.5).astype(jnp.bfloat16)
    return dict(dy_rows=dy_rows, hidden_rows=hidden_rows, row_counts=row_counts, hot_owner=hot_owner, master=master, moment1=moment1, moment2=moment2)


beta_one = 0.9
beta_two = 0.95
learn_rate = 0.00022
weight_decay = 0.1
epsilon = 1e-08
bias_one = 1.0 - 0.9 ** 10
bias_two = 1.0 - 0.95 ** 10

def adamw_update(master, moment1, moment2, gradient):
    first_moment = beta_one * moment1.astype(jnp.float32) + (1.0 - beta_one) * gradient
    second_moment = beta_two * moment2.astype(jnp.float32) + (1.0 - beta_two) * gradient * gradient
    direction = first_moment / bias_one / (jnp.sqrt(second_moment / bias_two) + epsilon)
    updated = master * (1.0 - learn_rate * weight_decay) - learn_rate * direction
    return (updated, first_moment.astype(jnp.bfloat16), second_moment.astype(jnp.bfloat16))

def slot_masks(counts, cap_rows):
    position = jnp.arange(cap_rows, dtype=jnp.int32)
    lower = counts[..., 0:1]
    upper = lower + counts[..., 1:2]
    return (position < lower, (position >= lower) & (position < upper))

def group_parts(pieces):
    dy_group, hidden_group, count_group = pieces
    gathered = dy_group.reshape(N_EXPERT, N_EXPERT, CAP, WIN).transpose(1, 0, 2, 3)
    gathered = gathered.reshape(N_EXPERT, N_EXPERT * CAP, WIN).astype(jnp.float32)
    mask_own, mask_hot = slot_masks(count_group, CAP)
    mask_own = mask_own.reshape(N_EXPERT, N_EXPERT * CAP, 1)
    mask_hot = mask_hot.reshape(N_EXPERT, N_EXPERT * CAP, 1)
    hidden_float = hidden_group.astype(jnp.float32)
    part_own = jnp.einsum('drp,drk->dpk', jnp.where(mask_own, hidden_float, 0.0), gathered)
    part_hot = jnp.einsum('drp,drk->dpk', jnp.where(mask_hot, hidden_float, 0.0), gathered)
    return (part_own, part_hot)

def reference(dy_rows, hidden_rows, row_counts, hot_owner, master, moment1, moment2):
    own_parts, hot_parts = lax.map(group_parts, (dy_rows, hidden_rows, row_counts))
    is_owner = jnp.arange(N_GROUP, dtype=jnp.int32)[:, None] == hot_owner[None, :]
    owner_mask = is_owner[:, :, None, None]
    hot_total = lax.optimization_barrier(jnp.sum(hot_parts, axis=0)) + lax.optimization_barrier(jnp.sum(jnp.where(owner_mask, own_parts, 0.0), axis=0))
    gradient = jnp.where(owner_mask, hot_total[None], own_parts)
    new_master, new_moment1, new_moment2 = adamw_update(master, moment1, moment2, gradient)
    replica = new_master[hot_owner, jnp.arange(N_EXPERT, dtype=jnp.int32)].astype(jnp.bfloat16)
    replica_panel = jnp.broadcast_to(replica[None], (N_GROUP, N_EXPERT, HID, WIN))
    return (new_master, new_moment1, new_moment2, replica_panel)
```

```python
import functools

import jax
import jax.numpy as jnp
from jax import lax
from jax.experimental import pallas as pl
from jax.experimental.pallas import tpu as pltpu
from jax.sharding import PartitionSpec as P

MESH = pl.DeviceIdType.MESH
F32, BF16 = jnp.float32, jnp.bfloat16

beta_one = 0.9
beta_two = 0.95
learn_rate = 0.00022
weight_decay = 0.1
epsilon = 1e-08
bias_one = 1.0 - 0.9**10
bias_two = 1.0 - 0.95**10

ROWS, HID, WIN, CAP = 768, 128, 3584, 24
WIDTHS = (512,) * 7
SPACING = 4
AHEAD = 2


def kernel(
    dy, hid, cnt, owner, master, moment1, moment2,
    out_master, out_m1, out_m2, out_rep,
    recv, hidden, hidden_f, left_f, left, x_out, x_in,
    prod, own_in, sib_in, rs_in, total, mst, m1, m2, rep, rep_in, rep_slices, rep_full,
    s_in, s_x, s_a, s_own, s_sib, s_rs, s_ag, s_fwd, s_g1, s_g2, s_g3, s_g4, s_out,
):
    g, e = lax.axis_index("group"), lax.axis_index("expert")
    zh, c = lax.div(g, 2), lax.rem(g, 2)
    xy, p = lax.div(e, 2), lax.rem(e, 2)
    x, y = lax.div(xy, 4), lax.rem(xy, 4)
    z = 2 * zh + p
    o = lax.rem(p + c, 2)
    sigma = 1 - 2 * c
    partner = (g, e + 1 - 2 * p)
    sibling = (g + 1 - 2 * c, e)

    def ring(step):
        zz = lax.rem(z + step + 8, 8)
        return (lax.div(zz, 2) * 2 + c, xy * 2 + lax.rem(zz, 2))

    def column(i):
        return lax.rem(zh + i, 4)

    def plane(dx, dy_):
        return lax.rem(x + dx, 4) * 4 + lax.rem(y + dy_, 4)

    starts = [sum(WIDTHS[:k]) for k in range(len(WIDTHS))]
    count = len(WIDTHS)
    cols = [pl.ds(s, w) for s, w in zip(starts, WIDTHS)]
    offsets = [(a, b) for a in range(4) for b in range(4) if (a, b) != (0, 0)]

    def remote(src, dst, sems, device):
        return pltpu.make_async_remote_copy(
            src_ref=src, dst_ref=dst, send_sem=sems[0], recv_sem=sems[1],
            device_id=device, device_id_type=MESH,
        )

    def pair(sems, *index):
        return sems.at[(0, *index)], sems.at[(1, *index)]

    loads = [
        pltpu.make_async_copy(hid.at[0, 0], hidden, s_in.at[0]),
        pltpu.make_async_copy(master.at[0, 0], mst, s_in.at[1]),
        pltpu.make_async_copy(moment1.at[0, 0], m1, s_in.at[2]),
        pltpu.make_async_copy(moment2.at[0, 0], m2, s_in.at[3]),
    ]
    for load in loads:
        load.start()

    barrier = pltpu.get_barrier_semaphore()
    peers = [(g, plane(a, b) * 2 + p) for a, b in offsets]
    peers += [sibling, ring(1), ring(-1)]
    peers += [(column(i) * 2 + c, e) for i in (1, 2, 3)]
    for peer in peers:
        pl.semaphore_signal(barrier, inc=1, device_id=peer, device_id_type=MESH)
    pl.semaphore_wait(barrier, len(peers))

    def rows_start(k):
        for a, b in offsets:
            there = plane(a, b)
            remote(
                dy.at[0, 0, pl.ds(pl.multiple_of(there * 48, 48), 48), cols[k]],
                recv.at[xy, :, cols[k]],
                pair(s_a, k),
                (g, there * 2 + p),
            ).start()
        pltpu.make_async_copy(
            dy.at[0, 0, pl.ds(pl.multiple_of(xy * 48, 48), 48), cols[k]],
            recv.at[xy, :, cols[k]],
            s_a.at[1, k],
        ).start()

    for k in range(min(AHEAD + 1, count)):
        rows_start(k)

    loads[0].wait()
    hidden_f[...] = hidden[...].astype(F32)
    left_f[...] = jnp.zeros_like(left_f)
    position = lax.broadcasted_iota(jnp.int32, (CAP, HID), 0)
    owns = owner[0] == g

    def masked(s):
        h = hidden_f[pl.ds(pl.multiple_of(s * CAP, 8), CAP), :]
        a = cnt[0, 0, s, 0]
        upper = a + cnt[0, 0, s, 1]
        lower = jnp.where(owns, 0, a)
        own = jnp.where(position < a, h, 0.0)
        hot = jnp.where((position >= lower) & (position < upper), h, 0.0)
        return own, hot

    def fill_out(i, carry):
        own, hot = masked(2 * i + 1 - p)
        at = pl.ds(pl.multiple_of(i * CAP, 8), CAP)
        x_out_f = left_f
        x_out_f[at, 0:HID] = own
        x_out_f[at, HID : 2 * HID] = hot
        return carry

    lax.fori_loop(0, 16, fill_out, 0)
    x_out[...] = left_f[0:384, 0:256].astype(BF16)
    send_x = remote(x_out, x_in, (s_x.at[0], s_x.at[1]), partner)
    send_x.start()
    left_f[...] = jnp.zeros_like(left_f)

    def fill_mine(i, carry):
        own, hot = masked(2 * i + p)
        at = pl.ds(pl.multiple_of(i * 48 + p * CAP, 8), CAP)
        left_f[at, 0:HID] = own
        left_f[at, 2 * HID : 3 * HID] = hot
        return carry

    lax.fori_loop(0, 16, fill_mine, 0)
    send_x.wait_recv()
    hidden_x = hidden_f
    for half in range(2):
        hidden_x[0:384, :] = x_in[:, half * HID : (half + 1) * HID].astype(F32)

        def fill_other(i, carry):
            at = pl.ds(pl.multiple_of(i * 48 + (1 - p) * CAP, 8), CAP)
            block = hidden_x[pl.ds(pl.multiple_of(i * CAP, 8), CAP), :]
            left_f[at, (2 * half + 1) * HID : (2 * half + 2) * HID] = block
            return carry

        lax.fori_loop(0, 16, fill_other, 0)
    for j in range(4):
        left[j * HID : (j + 1) * HID, :] = left_f[:, j * HID : (j + 1) * HID].T.astype(BF16)

    def rows_of(delta):
        home = lax.rem(z - sigma * delta + 16, 8)
        return pl.ds(pl.multiple_of(lax.div(home - c, 2) * 32, 32), 32)

    hot_mine = pl.ds(pl.multiple_of(2 * HID + HID * o, HID), HID)
    hot_other = pl.ds(pl.multiple_of(2 * HID + HID * (1 - o), HID), HID)
    here = pl.ds(pl.multiple_of(zh * 32, 32), 32)

    def own_copy(k):
        return remote(prod.at[HID : 2 * HID, cols[k]], own_in.at[:, cols[k]], pair(s_own, k), partner)

    def sib_copy(k):
        return remote(prod.at[hot_other, cols[k]], sib_in.at[:, cols[k]], pair(s_sib, k), sibling)

    toward = sigma * (2 * o - 1)

    def rs_copy(k, step):
        direction = (toward, -toward, toward, -sigma)[step]
        src = sib_in.at[rows_of(4 + o), cols[k]] if step == 0 else rs_in.at[step - 1, :, cols[k]]
        return remote(src, rs_in.at[step, :, cols[k]], pair(s_rs, k, step), ring(direction))

    def ag_copy(k, i):
        return remote(total.at[here, cols[k]], total.at[here, cols[k]], pair(s_ag, k, i - 1), (column(i) * 2 + c, e))

    def fwd_copy(k):
        return remote(total.at[:, cols[k]], total.at[:, cols[k]], pair(s_fwd, k), sibling)

    def g1_copy(k):
        return remote(rep.at[:, cols[k]], rep_in.at[:, cols[k]], pair(s_g1, k), sibling)

    def g2_copy(k, i):
        there = pl.ds(pl.multiple_of(column(i) * 32, 32), 32)
        return remote(rep.at[there, cols[k]], rep_slices.at[i - 1, :, cols[k]], pair(s_g2, k, i - 1), (column(i) * 2 + c, e))

    def g3_copy(k, i):
        return remote(rep_full.at[here, cols[k]], rep_full.at[here, cols[k]], pair(s_g3, k, i - 1), (column(i) * 2 + c, e))

    def g4_copy(k):
        return remote(rep_full.at[:, cols[k]], rep_full.at[:, cols[k]], pair(s_g4, k), sibling)

    def out_copy(k, n):
        src = (mst, m1, m2, rep_full)[n]
        dst = (out_master, out_m1, out_m2, out_rep)[n]
        return pltpu.make_async_copy(src.at[:, cols[k]], dst.at[0, 0, :, cols[k]], s_out.at[k, n])

    def product(k):
        pltpu.make_async_copy(recv.at[:, :, cols[k]], recv.at[:, :, cols[k]], s_a.at[1, k]).wait()
        if k + AHEAD + 1 < count:
            rows_start(k + AHEAD + 1)

        def block(n, carry):
            at = pl.ds(pl.multiple_of(starts[k] + n * 256, 256), 256)
            right = recv[:, :, at].reshape(ROWS, 256)
            for j in range(2):
                rows = pl.ds(j * 256, 256)
                prod[rows, at] = jnp.dot(left[rows, :], right, preferred_element_type=F32)
            return carry

        lax.fori_loop(0, WIDTHS[k] // 256, block, 0)
        sib_copy(k).start()
        own_copy(k).start()

    def chip_sum(k):
        sib_copy(k).wait_recv()
        sib_in[:, cols[k]] += prod[hot_mine, cols[k]]
        rs_copy(k, 0).start()

    def relay(step, delta):
        def run(k):
            rs_copy(k, step - 1).wait_recv()
            rs_in[step - 1, :, cols[k]] += sib_in[rows_of(delta), cols[k]]
            rs_copy(k, step).start()

        return run

    def last_relay(k):
        @pl.when(o == 1)
        def _():
            relay(3, 1)(k)

    def gather(k):
        @pl.when(o == 0)
        def _():
            rs_copy(k, 2).wait_recv()
            rs_copy(k, 3).wait_recv()
            total[here, cols[k]] = sib_in[here, cols[k]] + rs_in[2, :, cols[k]] + rs_in[3, :, cols[k]]
            for i in (2, 1, 3):
                ag_copy(k, i).start()

    def ag_wait(k, i, buffer, sems):
        there = pl.ds(pl.multiple_of(lax.rem(zh + 4 - i, 4) * 32, 32), 32)
        remote(buffer.at[there, cols[k]], buffer.at[there, cols[k]], pair(sems, k, i - 1), sibling).wait_recv()

    def forward(k):
        @pl.when(o == 0)
        def _():
            for i in (1, 3, 2):
                ag_wait(k, i, total, s_ag)
            fwd_copy(k).start()

    def update(k):
        if k == 0:
            for load in loads[1:]:
                load.wait()

        @pl.when(o == 1)
        def _():
            fwd_copy(k).wait_recv()

        own_copy(k).wait_recv()
        w = WIDTHS[k]

        def block(n, carry):
            at = (pl.ds(pl.multiple_of(n * 16, 16), 16), cols[k])
            mask = jnp.full((16, w), owner[0], jnp.int32) == jnp.full((16, w), g, jnp.int32)
            gradient = jnp.where(mask, total[at], prod[at] + own_in[at])
            first = beta_one * m1[at].astype(F32) + (1.0 - beta_one) * gradient
            second = beta_two * m2[at].astype(F32) + (1.0 - beta_two) * gradient * gradient
            direction = first / (bias_one * (jnp.sqrt(second * (1.0 / bias_two)) + epsilon))
            updated = mst[at] * (1.0 - learn_rate * weight_decay) - learn_rate * direction
            mst[at] = updated
            m1[at] = first.astype(BF16)
            m2[at] = second.astype(BF16)
            rep[at] = jnp.where(mask, updated, 0.0).astype(BF16)
            return carry

        lax.fori_loop(0, 8, block, 0)

        @pl.when(o == 1)
        def _():
            g1_copy(k).start()

        for n in range(3):
            out_copy(k, n).start()

    def scatter(k):
        @pl.when(o == 0)
        def _():
            g1_copy(k).wait_recv()
            rep[:, cols[k]] += rep_in[:, cols[k]]
            for i in (2, 1, 3):
                g2_copy(k, i).start()

    def regather(k):
        @pl.when(o == 0)
        def _():
            for i in (1, 3, 2):
                g2_copy(k, i).wait_recv()
            rep_full[here, cols[k]] = (rep[here, cols[k]] + rep_slices[0, :, cols[k]]) + (
                rep_slices[1, :, cols[k]] + rep_slices[2, :, cols[k]]
            )
            for i in (2, 1, 3):
                g3_copy(k, i).start()

    def share(k):
        @pl.when(o == 0)
        def _():
            for i in (1, 3, 2):
                ag_wait(k, i, rep_full, s_g3)
            g4_copy(k).start()

    def finish(k):
        @pl.when(o == 1)
        def _():
            g4_copy(k).wait_recv()

        out_copy(k, 3).start()

    stages = [
        product, chip_sum, relay(1, 6 - 3 * o), relay(2, 2 + 5 * o), last_relay, gather,
        forward, update, scatter, regather, share, finish,
    ]
    order = sorted(
        (SPACING * k + i, -k, i) for k in range(count) for i in range(len(stages))
    )
    for _, minus, i in order:
        stages[i](-minus)

    send_x.wait_send()
    for k in range(count):
        half = recv.at[0:15, :, cols[k]]
        remote(half, half, pair(s_a, k), sibling).wait_send()
        own_copy(k).wait_send()
        sib_copy(k).wait_send()
        for step in range(3):
            rs_copy(k, step).wait_send()

        @pl.when(o == 1)
        def _():
            rs_copy(k, 3).wait_send()
            g1_copy(k).wait_send()

        @pl.when(o == 0)
        def _():
            for i in (1, 2, 3):
                ag_copy(k, i).wait_send()
                g2_copy(k, i).wait_send()
                g3_copy(k, i).wait_send()
            fwd_copy(k).wait_send()
            g4_copy(k).wait_send()

        for n in range(4):
            out_copy(k, n).wait()


def local(dy_rows, hidden_rows, row_counts, hot_owner, master, moment1, moment2):
    count = len(WIDTHS)
    dma = pltpu.SemaphoreType.DMA
    anywhere = pl.BlockSpec(memory_space=pl.ANY)
    scalars = pl.BlockSpec(memory_space=pltpu.SMEM)
    return pl.pallas_call(
        kernel,
        name="expert_grad",
        out_shape=(
            jax.ShapeDtypeStruct((1, 1, HID, WIN), F32),
            jax.ShapeDtypeStruct((1, 1, HID, WIN), BF16),
            jax.ShapeDtypeStruct((1, 1, HID, WIN), BF16),
            jax.ShapeDtypeStruct((1, 1, HID, WIN), BF16),
        ),
        in_specs=[anywhere, anywhere, scalars, scalars, anywhere, anywhere, anywhere],
        out_specs=(anywhere,) * 4,
        scratch_shapes=[
            pltpu.VMEM((16, 48, WIN), BF16),
            pltpu.VMEM((ROWS, HID), BF16),
            pltpu.VMEM((ROWS, HID), F32),
            pltpu.VMEM((ROWS, 4 * HID), F32),
            pltpu.VMEM((4 * HID, ROWS), BF16),
            pltpu.VMEM((ROWS // 2, 2 * HID), BF16),
            pltpu.VMEM((ROWS // 2, 2 * HID), BF16),
            pltpu.VMEM((4 * HID, WIN), F32),
            pltpu.VMEM((HID, WIN), F32),
            pltpu.VMEM((HID, WIN), F32),
            pltpu.VMEM((4, 32, WIN), F32),
            pltpu.VMEM((HID, WIN), F32),
            pltpu.VMEM((HID, WIN), F32),
            pltpu.VMEM((HID, WIN), BF16),
            pltpu.VMEM((HID, WIN), BF16),
            pltpu.VMEM((HID, WIN), BF16),
            pltpu.VMEM((HID, WIN), BF16),
            pltpu.VMEM((3, 32, WIN), BF16),
            pltpu.VMEM((HID, WIN), BF16),
            dma((4,)),
            dma((2,)),
            dma((2, count)),
            dma((2, count)),
            dma((2, count)),
            dma((2, count, 4)),
            dma((2, count, 3)),
            dma((2, count)),
            dma((2, count)),
            dma((2, count, 3)),
            dma((2, count, 3)),
            dma((2, count)),
            dma((count, 4)),
        ],
        compiler_params=pltpu.CompilerParams(
            collective_id=0, has_side_effects=True, vmem_limit_bytes=56 * 2**20
        ),
        cost_estimate=pl.CostEstimate(
            flops=2 * 4 * HID * ROWS * WIN, bytes_accessed=16 * 2**20, transcendentals=HID * WIN
        ),
    )(dy_rows, hidden_rows, row_counts, hot_owner, master, moment1, moment2)


def solution(mesh):
    rows = P("group", "expert", None, None)
    return jax.shard_map(
        local,
        mesh=mesh,
        in_specs=(rows, rows, rows, P("expert"), rows, rows, rows),
        out_specs=(rows,) * 4,
        check_vma=False,
    )
```

```python
import functools

import jax
import jax.numpy as jnp
from jax import lax
from jax.experimental import pallas as pl
from jax.experimental.pallas import tpu as pltpu
from jax.sharding import PartitionSpec as P

MESH = pl.DeviceIdType.MESH
F32, BF16, I16 = jnp.float32, jnp.bfloat16, jnp.int16

beta_one = 0.9
beta_two = 0.95
learn_rate = 0.00022
weight_decay = 0.1
epsilon = 1e-08
bias_one = 1.0 - 0.9**10
bias_two = 1.0 - 0.95**10

ROWS, HID, WIN, CAP = 768, 128, 3584, 24
WIDTHS = (256,) * 14
SPACING = 1
NEWEST = 1
AHEAD = 2


def coded(value):
    peak = jnp.maximum(jnp.max(jnp.abs(value), axis=0, keepdims=True), 1e-30)
    code = jnp.round(value * (32767.0 / peak)).astype(jnp.int32).astype(jnp.int16)
    return code, peak * (1.0 / 32767.0)


def decoded(code, step):
    return code.astype(jnp.int32).astype(F32) * step


def kernel(
    dy, hid, cnt, owner, master, moment1, moment2,
    mst, m1, m2, rep_full,
    recv, hidden, hidden_f, left_f, left, x_out, x_in,
    prod, own_q, own_s, own_qi, own_si, sib_in, ring_q, ring_s, ring_qi, ring_si, rs_q, rs_s, rs_qi, rs_si, total_q, total_s,
    sib_mst, sib_m1, sib_m2, rep, rep_slices,
    s_in, s_state, s_x, s_a, s_own, s_sib, s_ring, s_rs, s_ag, s_fwd, s_g2, s_g3, s_g4,
):
    mst, m1, m2, rep_full = (ref.at[0, 0] for ref in (mst, m1, m2, rep_full))
    g, e = lax.axis_index("group"), lax.axis_index("expert")
    zh, c = lax.div(g, 2), lax.rem(g, 2)
    xy, p = lax.div(e, 2), lax.rem(e, 2)
    x, y = lax.div(xy, 4), lax.rem(xy, 4)
    z = 2 * zh + p
    o = lax.rem(p + c, 2)
    sigma = 1 - 2 * c
    partner = (g, e + 1 - 2 * p)
    sibling = (g + 1 - 2 * c, e)

    def ring(step):
        zz = lax.rem(z + step + 8, 8)
        return (lax.div(zz, 2) * 2 + c, xy * 2 + lax.rem(zz, 2))

    def column(i):
        return lax.rem(zh + i, 4)

    def plane(dx, dy_):
        return lax.rem(x + dx, 4) * 4 + lax.rem(y + dy_, 4)

    starts = [sum(WIDTHS[:k]) for k in range(len(WIDTHS))]
    count = len(WIDTHS)
    cols = [pl.ds(s, w) for s, w in zip(starts, WIDTHS)]
    offsets = [(a, b) for a in range(4) for b in range(4) if (a, b) != (0, 0)]

    def remote(src, dst, sems, device):
        return pltpu.make_async_remote_copy(
            src_ref=src, dst_ref=dst, send_sem=sems[0], recv_sem=sems[1],
            device_id=device, device_id_type=MESH,
        )

    def pair(sems, *index):
        return sems.at[(0, *index)], sems.at[(1, *index)]

    loads = [
        pltpu.make_async_copy(hid.at[0, 0], hidden, s_in.at[0]),
        pltpu.make_async_copy(master.at[0, 0], mst, s_in.at[1]),
        pltpu.make_async_copy(moment1.at[0, 0], m1, s_in.at[2]),
        pltpu.make_async_copy(moment2.at[0, 0], m2, s_in.at[3]),
    ]
    for load in loads:
        load.start()

    barrier = pltpu.get_barrier_semaphore()
    peers = [(g, plane(a, b) * 2 + p) for a, b in offsets]
    peers += [sibling, ring(1), ring(-1)]
    peers += [(column(i) * 2 + c, e) for i in (1, 2, 3)]
    for peer in peers:
        pl.semaphore_signal(barrier, inc=1, device_id=peer, device_id_type=MESH)
    pl.semaphore_wait(barrier, len(peers))

    def rows_start(k):
        for a, b in offsets:
            there = plane(a, b)
            remote(
                dy.at[0, 0, pl.ds(pl.multiple_of(there * 48, 48), 48), cols[k]],
                recv.at[xy, :, cols[k]],
                pair(s_a, k),
                (g, there * 2 + p),
            ).start()
        pltpu.make_async_copy(
            dy.at[0, 0, pl.ds(pl.multiple_of(xy * 48, 48), 48), cols[k]],
            recv.at[xy, :, cols[k]],
            s_a.at[1, k],
        ).start()

    rows_start(0)

    states = [
        remote(src.at[0, 0], dst, pair(s_state, n), sibling)
        for n, (src, dst) in enumerate(((master, sib_mst), (moment1, sib_m1), (moment2, sib_m2)))
    ]

    loads[0].wait()
    hidden_f[...] = hidden[...].astype(F32)
    left_f[...] = jnp.zeros_like(left_f)
    position = lax.broadcasted_iota(jnp.int32, (CAP, HID), 0)
    owns = owner[0] == g

    def masked(s):
        h = hidden_f[pl.ds(pl.multiple_of(s * CAP, 8), CAP), :]
        a = cnt[0, 0, 0, s]
        upper = a + cnt[0, 0, 1, s]
        lower = jnp.where(owns, 0, a)
        own = jnp.where(position < a, h, 0.0)
        hot = jnp.where((position >= lower) & (position < upper), h, 0.0)
        return own, hot

    def fill_out(i, carry):
        own, hot = masked(2 * i + 1 - p)
        at = pl.ds(pl.multiple_of(i * CAP, 8), CAP)
        x_out_f = left_f
        x_out_f[at, 0:HID] = own
        x_out_f[at, HID : 2 * HID] = hot
        return carry

    lax.fori_loop(0, 16, fill_out, 0)
    x_out[...] = left_f[0:384, 0:256].astype(BF16)
    send_x = remote(x_out, x_in, (s_x.at[0], s_x.at[1]), partner)
    send_x.start()
    for k in range(1, min(AHEAD + 1, count)):
        rows_start(k)
    @pl.when(o == 1)
    def _():
        for copy in states:
            copy.start()

    left_f[...] = jnp.zeros_like(left_f)

    def fill_mine(i, carry):
        own, hot = masked(2 * i + p)
        at = pl.ds(pl.multiple_of(i * 48 + p * CAP, 8), CAP)
        left_f[at, 0:HID] = own
        left_f[at, 2 * HID : 3 * HID] = hot
        return carry

    lax.fori_loop(0, 16, fill_mine, 0)
    send_x.wait_recv()
    hidden_x = hidden_f
    for half in range(2):
        hidden_x[0:384, :] = x_in[:, half * HID : (half + 1) * HID].astype(F32)

        def fill_other(i, carry):
            at = pl.ds(pl.multiple_of(i * 48 + (1 - p) * CAP, 8), CAP)
            block = hidden_x[pl.ds(pl.multiple_of(i * CAP, 8), CAP), :]
            left_f[at, (2 * half + 1) * HID : (2 * half + 2) * HID] = block
            return carry

        lax.fori_loop(0, 16, fill_other, 0)
    for j in range(4):
        left[j * HID : (j + 1) * HID, :] = left_f[:, j * HID : (j + 1) * HID].T.astype(BF16)

    hot_mine = pl.ds(pl.multiple_of(HID + HID * o, HID), HID)
    hot_other = pl.ds(pl.multiple_of(HID + HID * (1 - o), HID), HID)
    here = pl.ds(pl.multiple_of(zh * 32, 32), 32)

    def each(copies, what):
        for copy in copies:
            getattr(copy, what)()

    def own_copy(k):
        return (
            remote(own_q.at[:, cols[k]], own_qi.at[:, cols[k]], pair(s_own, k, 0), partner),
            remote(own_s.at[:, cols[k]], own_si.at[:, cols[k]], pair(s_own, k, 1), partner),
        )

    def sib_copy(k):
        return remote(prod.at[hot_other, cols[k]], sib_in.at[:, cols[k]], pair(s_sib, k), sibling)

    def rows_at(i):
        return pl.ds(pl.multiple_of(i * 32, 32), 32)

    def ring_copy(k):
        return (
            remote(ring_q.at[:, cols[k]], ring_qi.at[:, cols[k]], pair(s_ring, k, 0), ring(sigma)),
            remote(ring_s.at[:, cols[k]], ring_si.at[:, cols[k]], pair(s_ring, k, 1), ring(sigma)),
        )

    def rs_copy(k, i):
        j = column(i)
        there = (j * 2 + c, e)
        return (
            remote(rs_q.at[rows_at(j), cols[k]], rs_qi.at[i - 1, :, cols[k]], pair(s_rs, k, i - 1, 0), there),
            remote(rs_s.at[j, :, cols[k]], rs_si.at[i - 1, :, cols[k]], pair(s_rs, k, i - 1, 1), there),
        )

    def ag_copy(k, i):
        there = (column(i) * 2 + c, e)
        return (
            remote(total_q.at[here, cols[k]], total_q.at[here, cols[k]], pair(s_ag, k, i - 1, 0), there),
            remote(total_s.at[zh, :, cols[k]], total_s.at[zh, :, cols[k]], pair(s_ag, k, i - 1, 1), there),
        )

    def fwd_copy(k):
        return (
            remote(total_q.at[:, cols[k]], total_q.at[:, cols[k]], pair(s_fwd, k, 0), sibling),
            remote(total_s.at[:, :, cols[k]], total_s.at[:, :, cols[k]], pair(s_fwd, k, 1), sibling),
        )

    def g2_copy(k, i):
        there = pl.ds(pl.multiple_of(column(i) * 32, 32), 32)
        return remote(rep.at[there, cols[k]], rep_slices.at[i - 1, :, cols[k]], pair(s_g2, k, i - 1), (column(i) * 2 + c, e))

    def g3_copy(k, i):
        return remote(rep_full.at[here, cols[k]], rep_full.at[here, cols[k]], pair(s_g3, k, i - 1), (column(i) * 2 + c, e))

    def g4_copy(k):
        return remote(rep_full.at[:, cols[k]], rep_full.at[:, cols[k]], pair(s_g4, k), sibling)

    def tiles(k, body):
        wide = 256 if WIDTHS[k] % 256 == 0 else 128

        def block(n, carry):
            body(pl.ds(pl.multiple_of(starts[k] + n * wide, 128), wide))
            return carry

        lax.fori_loop(0, WIDTHS[k] // wide, block, 0)

    def product(k):
        pltpu.make_async_copy(recv.at[:, :, cols[k]], recv.at[:, :, cols[k]], s_a.at[1, k]).wait()
        if k + AHEAD + 1 < count:
            rows_start(k + AHEAD + 1)

        def body(at):
            right = recv[:, :, at].reshape(ROWS, at.size)
            own = jnp.dot(left[0 : 2 * HID, :], right, preferred_element_type=F32)
            prod[0:HID, at] = own[0:HID]
            own_q[:, at], own_s[:, at] = coded(own[HID:])
            prod[HID:, at] = jnp.dot(left[2 * HID :, :], right, preferred_element_type=F32)

        tiles(k, body)
        sib_copy(k).start()
        each(own_copy(k), "start")

    def chip_sum(k):
        sib_copy(k).wait_recv()
        sib_in[:, cols[k]] += prod[hot_mine, cols[k]]

        @pl.when(o == 1)
        def _():
            def body(at):
                ring_q[:, at], ring_s[:, at] = coded(sib_in[:, at])

            tiles(k, body)
            each(ring_copy(k), "start")

    def scatter(k):
        @pl.when(o == 0)
        def _():
            each(ring_copy(k), "wait_recv")

            def body(at):
                for j in range(4):
                    rows = pl.ds(j * 32, 32)
                    part = sib_in[rows, at] + decoded(ring_qi[rows, at], ring_si[:, at])
                    sib_in[rows, at] = part
                    rs_q[rows, at], rs_s[j, :, at] = coded(part)

            tiles(k, body)
            for i in (2, 1, 3):
                each(rs_copy(k, i), "start")

    def gather(k):
        @pl.when(o == 0)
        def _():
            for i in (1, 3, 2):
                each(rs_copy(k, i), "wait_recv")

            def body(at):
                part = sib_in[here, at]
                for i in range(3):
                    part = part + decoded(rs_qi[i, :, at], rs_si[i, :, at])
                total_q[here, at], total_s[zh, :, at] = coded(part)

            tiles(k, body)
            for i in (2, 1, 3):
                each(ag_copy(k, i), "start")

    def ag_wait(k, i, buffer, sems):
        there = pl.ds(pl.multiple_of(lax.rem(zh + 4 - i, 4) * 32, 32), 32)
        remote(buffer.at[there, cols[k]], buffer.at[there, cols[k]], pair(sems, k, i - 1), sibling).wait_recv()

    def adamw(old, first_old, second_old, gradient):
        first = beta_one * first_old.astype(F32) + (1.0 - beta_one) * gradient
        second = beta_two * second_old.astype(F32) + (1.0 - beta_two) * gradient * gradient
        direction = first / (bias_one * (jnp.sqrt(second * (1.0 / bias_two)) + epsilon))
        updated = old * (1.0 - learn_rate * weight_decay) - learn_rate * direction
        return updated, first.astype(BF16), second.astype(BF16)

    def belongs(group, w):
        return jnp.full((16, w), owner[0], jnp.int32) == jnp.full((16, w), group, jnp.int32)

    def blocks(k, body):
        def block(n, carry):
            at = (pl.ds(pl.multiple_of(n * 16, 16), 16), cols[k])
            body(at, decoded(total_q[at], total_s[lax.div(n, 2), :, cols[k]]))
            return carry

        lax.fori_loop(0, 8, block, 0)

    def replicate(k):
        if k == 0:
            for load in loads[1:]:
                load.wait()

        @pl.when(o == 0)
        def _():
            if k == 0:
                each(states, "wait_recv")
            for i in (1, 3, 2):
                frm = lax.rem(zh + 4 - i, 4)
                block = total_q.at[rows_at(frm), cols[k]]
                steps = total_s.at[frm, :, cols[k]]
                remote(block, block, pair(s_ag, k, i - 1, 0), sibling).wait_recv()
                remote(steps, steps, pair(s_ag, k, i - 1, 1), sibling).wait_recv()
            each(fwd_copy(k), "start")

            def body(at, hot):
                mine, other = belongs(g, WIDTHS[k]), belongs(sibling[0], WIDTHS[k])
                updated, _, _ = adamw(
                    jnp.where(mine, mst[at], sib_mst[at]),
                    jnp.where(mine, m1[at].astype(F32), sib_m1[at].astype(F32)),
                    jnp.where(mine, m2[at].astype(F32), sib_m2[at].astype(F32)),
                    hot,
                )
                rep[at] = jnp.where(mine | other, updated, 0.0).astype(BF16)

            blocks(k, body)
            for i in (2, 1, 3):
                g2_copy(k, i).start()

    def update(k):
        @pl.when(o == 1)
        def _():
            each(fwd_copy(k), "wait_recv")

        each(own_copy(k), "wait_recv")

        def body(at, hot):
            own = prod[at] + decoded(own_qi[at], own_si[:, cols[k]])
            gradient = jnp.where(belongs(g, WIDTHS[k]), hot, own)
            mst[at], m1[at], m2[at] = adamw(mst[at], m1[at], m2[at], gradient)

        blocks(k, body)

    def regather(k):
        @pl.when(o == 0)
        def _():
            for i in (1, 3, 2):
                g2_copy(k, i).wait_recv()
            rep_full[here, cols[k]] = (rep[here, cols[k]] + rep_slices[0, :, cols[k]]) + (
                rep_slices[1, :, cols[k]] + rep_slices[2, :, cols[k]]
            )
            for i in (2, 1, 3):
                g3_copy(k, i).start()

    def share(k):
        @pl.when(o == 0)
        def _():
            for i in (1, 3, 2):
                ag_wait(k, i, rep_full, s_g3)
            g4_copy(k).start()

    def finish(k):
        @pl.when(o == 1)
        def _():
            g4_copy(k).wait_recv()


    stages = [product, chip_sum, scatter, gather, replicate, regather, share, update, finish]
    order = sorted(
        (SPACING * k + i, -k * NEWEST, i, k) for k in range(count) for i in range(len(stages))
    )
    for _, _, i, k in order:
        stages[i](k)

    send_x.wait_send()
    for k in range(count):
        half = recv.at[0:15, :, cols[k]]
        remote(half, half, pair(s_a, k), sibling).wait_send()
        each(own_copy(k), "wait_send")
        sib_copy(k).wait_send()

        @pl.when(o == 1)
        def _():
            if k == 0:
                each(states, "wait_send")
            each(ring_copy(k), "wait_send")

        @pl.when(o == 0)
        def _():
            for i in (1, 2, 3):
                each(rs_copy(k, i), "wait_send")
                each(ag_copy(k, i), "wait_send")
                g2_copy(k, i).wait_send()
                g3_copy(k, i).wait_send()
            each(fwd_copy(k), "wait_send")
            g4_copy(k).wait_send()


def local(dy_rows, hidden_rows, row_counts, hot_owner, master, moment1, moment2):
    count = len(WIDTHS)
    dma = pltpu.SemaphoreType.DMA
    in_hbm = pl.BlockSpec(memory_space=pltpu.HBM)
    scalars = pl.BlockSpec(memory_space=pltpu.SMEM)
    return pl.pallas_call(
        kernel,
        name="expert_grad",
        out_shape=(
            pltpu.VMEM((1, 1, HID, WIN), F32),
            pltpu.VMEM((1, 1, HID, WIN), BF16),
            pltpu.VMEM((1, 1, HID, WIN), BF16),
            pltpu.VMEM((1, 1, HID, WIN), BF16),
        ),
        in_specs=[in_hbm, in_hbm, scalars, scalars, in_hbm, in_hbm, in_hbm],
        out_specs=(pl.BlockSpec(memory_space=pltpu.VMEM),) * 4,
        scratch_shapes=[
            pltpu.VMEM((16, 48, WIN), BF16),
            pltpu.VMEM((ROWS, HID), BF16),
            pltpu.VMEM((ROWS, HID), F32),
            pltpu.VMEM((ROWS, 4 * HID), F32),
            pltpu.VMEM((4 * HID, ROWS), BF16),
            pltpu.VMEM((ROWS // 2, 2 * HID), BF16),
            pltpu.VMEM((ROWS // 2, 2 * HID), BF16),
            pltpu.VMEM((3 * HID, WIN), F32),
            pltpu.VMEM((HID, WIN), I16),
            pltpu.VMEM((1, WIN), F32),
            pltpu.VMEM((HID, WIN), I16),
            pltpu.VMEM((1, WIN), F32),
            pltpu.VMEM((HID, WIN), F32),
            pltpu.VMEM((HID, WIN), I16),
            pltpu.VMEM((1, WIN), F32),
            pltpu.VMEM((HID, WIN), I16),
            pltpu.VMEM((1, WIN), F32),
            pltpu.VMEM((HID, WIN), I16),
            pltpu.VMEM((4, 1, WIN), F32),
            pltpu.VMEM((3, 32, WIN), I16),
            pltpu.VMEM((3, 1, WIN), F32),
            pltpu.VMEM((HID, WIN), I16),
            pltpu.VMEM((4, 1, WIN), F32),
            pltpu.VMEM((HID, WIN), F32),
            pltpu.VMEM((HID, WIN), BF16),
            pltpu.VMEM((HID, WIN), BF16),
            pltpu.VMEM((HID, WIN), BF16),
            pltpu.VMEM((3, 32, WIN), BF16),
            dma((4,)),
            dma((2, 3)),
            dma((2,)),
            dma((2, count)),
            dma((2, count, 2)),
            dma((2, count)),
            dma((2, count, 2)),
            dma((2, count, 3, 2)),
            dma((2, count, 3, 2)),
            dma((2, count, 2)),
            dma((2, count, 3)),
            dma((2, count, 3)),
            dma((2, count)),
        ],
        compiler_params=pltpu.CompilerParams(
            collective_id=0, has_side_effects=True, vmem_limit_bytes=52 * 2**20
        ),
        cost_estimate=pl.CostEstimate(
            flops=2 * 4 * HID * ROWS * WIN, bytes_accessed=16 * 2**20, transcendentals=HID * WIN
        ),
    )(dy_rows, hidden_rows, jnp.swapaxes(row_counts, 2, 3), hot_owner, master, moment1, moment2)


def solution(mesh):
    rows = P("group", "expert", None, None)
    return jax.shard_map(
        local,
        mesh=mesh,
        in_specs=(rows, rows, rows, P("expert"), rows, rows, rows),
        out_specs=(rows,) * 4,
        check_vma=False,
    )
```

```python
import functools

import jax
import jax.numpy as jnp
from jax import lax
from jax.experimental import pallas as pl
from jax.experimental.pallas import tpu as pltpu
from jax.sharding import PartitionSpec as P

MESH = pl.DeviceIdType.MESH
F32, BF16, I16 = jnp.float32, jnp.bfloat16, jnp.int16

beta_one = 0.9
beta_two = 0.95
learn_rate = 0.00022
weight_decay = 0.1
epsilon = 1e-08
bias_one = 1.0 - 0.9**10
bias_two = 1.0 - 0.95**10

ROWS, HID, WIN, CAP = 768, 128, 3584, 24
WIDTHS = (256,) * 12 + (512,)
STATE_AT = 2
SPACING = 1
NEWEST = 1
AHEAD = 2


def coded(value):
    peak = jnp.maximum(jnp.max(jnp.abs(value), axis=0, keepdims=True), 1e-30)
    code = jnp.round(value * (32767.0 / peak)).astype(jnp.int32).astype(jnp.int16)
    return code, peak * (1.0 / 32767.0)


def decoded(code, step):
    return code.astype(jnp.int32).astype(F32) * step


def kernel(
    dy, hid, cnt, owner, master, moment1, moment2,
    mst, m1, m2, rep_full,
    recv, hidden, hidden_f, left_f, left, x_out, x_in,
    prod, own_q, own_s, own_qi, own_si, sib_in, ring_q, ring_s, ring_qi, ring_si, rs_q, rs_s, rs_qi, rs_si, total_q, total_s,
    sib_mst, sib_m1, sib_m2, rep, rep_slices,
    s_in, s_state, s_x, s_a, s_own, s_sib, s_ring, s_rs, s_ag, s_fwd, s_g2, s_g3, s_g4,
):
    mst, m1, m2, rep_full = (ref.at[0, 0] for ref in (mst, m1, m2, rep_full))
    g, e = lax.axis_index("group"), lax.axis_index("expert")
    zh, c = lax.div(g, 2), lax.rem(g, 2)
    xy, p = lax.div(e, 2), lax.rem(e, 2)
    x, y = lax.div(xy, 4), lax.rem(xy, 4)
    z = 2 * zh + p
    o = lax.rem(p + c, 2)
    sigma = 1 - 2 * c
    partner = (g, e + 1 - 2 * p)
    sibling = (g + 1 - 2 * c, e)

    def ring(step):
        zz = lax.rem(z + step + 8, 8)
        return (lax.div(zz, 2) * 2 + c, xy * 2 + lax.rem(zz, 2))

    def column(i):
        return lax.rem(zh + i, 4)

    def plane(dx, dy_):
        return lax.rem(x + dx, 4) * 4 + lax.rem(y + dy_, 4)

    starts = [sum(WIDTHS[:k]) for k in range(len(WIDTHS))]
    count = len(WIDTHS)
    cols = [pl.ds(s, w) for s, w in zip(starts, WIDTHS)]
    offsets = [(a, b) for a in range(4) for b in range(4) if (a, b) != (0, 0)]

    def remote(src, dst, sems, device):
        return pltpu.make_async_remote_copy(
            src_ref=src, dst_ref=dst, send_sem=sems[0], recv_sem=sems[1],
            device_id=device, device_id_type=MESH,
        )

    def pair(sems, *index):
        return sems.at[(0, *index)], sems.at[(1, *index)]

    loads = [
        pltpu.make_async_copy(hid.at[0, 0], hidden, s_in.at[0]),
        pltpu.make_async_copy(master.at[0, 0], mst, s_in.at[1]),
        pltpu.make_async_copy(moment1.at[0, 0], m1, s_in.at[2]),
        pltpu.make_async_copy(moment2.at[0, 0], m2, s_in.at[3]),
    ]
    loads[0].start()

    barrier = pltpu.get_barrier_semaphore()
    peers = [(g, plane(a, b) * 2 + p) for a, b in offsets]
    peers += [sibling, ring(1), ring(-1)]
    peers += [(column(i) * 2 + c, e) for i in (1, 2, 3)]
    for peer in peers:
        pl.semaphore_signal(barrier, inc=1, device_id=peer, device_id_type=MESH)
    pl.semaphore_wait(barrier, len(peers))

    def rows_start(k):
        for a, b in offsets:
            there = plane(a, b)
            remote(
                dy.at[0, 0, pl.ds(pl.multiple_of(there * 48, 48), 48), cols[k]],
                recv.at[xy, :, cols[k]],
                pair(s_a, k),
                (g, there * 2 + p),
            ).start()
        pltpu.make_async_copy(
            dy.at[0, 0, pl.ds(pl.multiple_of(xy * 48, 48), 48), cols[k]],
            recv.at[xy, :, cols[k]],
            s_a.at[1, k],
        ).start()

    rows_start(0)

    states = [
        remote(src.at[0, 0], dst, pair(s_state, n), sibling)
        for n, (src, dst) in enumerate(((master, sib_mst), (moment1, sib_m1), (moment2, sib_m2)))
    ]

    loads[0].wait()
    hidden_f[...] = hidden[...].astype(F32)
    left_f[...] = jnp.zeros_like(left_f)
    position = lax.broadcasted_iota(jnp.int32, (CAP, HID), 0)
    owns = owner[0] == g

    def masked(s):
        h = hidden_f[pl.ds(pl.multiple_of(s * CAP, 8), CAP), :]
        a = cnt[0, 0, 0, s]
        upper = a + cnt[0, 0, 1, s]
        lower = jnp.where(owns, 0, a)
        own = jnp.where(position < a, h, 0.0)
        hot = jnp.where((position >= lower) & (position < upper), h, 0.0)
        return own, hot

    def fill_out(i, carry):
        own, hot = masked(2 * i + 1 - p)
        at = pl.ds(pl.multiple_of(i * CAP, 8), CAP)
        x_out_f = left_f
        x_out_f[at, 0:HID] = own
        x_out_f[at, HID : 2 * HID] = hot
        return carry

    lax.fori_loop(0, 16, fill_out, 0)
    x_out[...] = left_f[0:384, 0:256].astype(BF16)
    send_x = remote(x_out, x_in, (s_x.at[0], s_x.at[1]), partner)
    send_x.start()
    for k in range(1, min(AHEAD + 1, count)):
        rows_start(k)

    left_f[...] = jnp.zeros_like(left_f)

    def fill_mine(i, carry):
        own, hot = masked(2 * i + p)
        at = pl.ds(pl.multiple_of(i * 48 + p * CAP, 8), CAP)
        left_f[at, 0:HID] = own
        left_f[at, 2 * HID : 3 * HID] = hot
        return carry

    lax.fori_loop(0, 16, fill_mine, 0)
    send_x.wait_recv()
    hidden_x = hidden_f
    for half in range(2):
        hidden_x[0:384, :] = x_in[:, half * HID : (half + 1) * HID].astype(F32)

        def fill_other(i, carry):
            at = pl.ds(pl.multiple_of(i * 48 + (1 - p) * CAP, 8), CAP)
            block = hidden_x[pl.ds(pl.multiple_of(i * CAP, 8), CAP), :]
            left_f[at, (2 * half + 1) * HID : (2 * half + 2) * HID] = block
            return carry

        lax.fori_loop(0, 16, fill_other, 0)
    for j in range(4):
        left[j * HID : (j + 1) * HID, :] = left_f[:, j * HID : (j + 1) * HID].T.astype(BF16)

    hot_mine = pl.ds(pl.multiple_of(HID + HID * o, HID), HID)
    hot_other = pl.ds(pl.multiple_of(HID + HID * (1 - o), HID), HID)
    here = pl.ds(pl.multiple_of(zh * 32, 32), 32)

    def each(copies, what):
        for copy in copies:
            getattr(copy, what)()

    def own_copy(k):
        return (
            remote(own_q.at[:, cols[k]], own_qi.at[:, cols[k]], pair(s_own, k, 0), partner),
            remote(own_s.at[:, cols[k]], own_si.at[:, cols[k]], pair(s_own, k, 1), partner),
        )

    def sib_copy(k):
        return remote(prod.at[hot_other, cols[k]], sib_in.at[:, cols[k]], pair(s_sib, k), sibling)

    def rows_at(i):
        return pl.ds(pl.multiple_of(i * 32, 32), 32)

    def ring_copy(k):
        return (
            remote(ring_q.at[:, cols[k]], ring_qi.at[:, cols[k]], pair(s_ring, k, 0), ring(sigma)),
            remote(ring_s.at[:, cols[k]], ring_si.at[:, cols[k]], pair(s_ring, k, 1), ring(sigma)),
        )

    def rs_copy(k, i):
        j = column(i)
        there = (j * 2 + c, e)
        return (
            remote(rs_q.at[rows_at(j), cols[k]], rs_qi.at[i - 1, :, cols[k]], pair(s_rs, k, i - 1, 0), there),
            remote(rs_s.at[j, :, cols[k]], rs_si.at[i - 1, :, cols[k]], pair(s_rs, k, i - 1, 1), there),
        )

    def ag_copy(k, i):
        there = (column(i) * 2 + c, e)
        return (
            remote(total_q.at[here, cols[k]], total_q.at[here, cols[k]], pair(s_ag, k, i - 1, 0), there),
            remote(total_s.at[zh, :, cols[k]], total_s.at[zh, :, cols[k]], pair(s_ag, k, i - 1, 1), there),
        )

    def fwd_copy(k):
        return (
            remote(total_q.at[:, cols[k]], total_q.at[:, cols[k]], pair(s_fwd, k, 0), sibling),
            remote(total_s.at[:, :, cols[k]], total_s.at[:, :, cols[k]], pair(s_fwd, k, 1), sibling),
        )

    def g2_copy(k, i):
        there = pl.ds(pl.multiple_of(column(i) * 32, 32), 32)
        return remote(rep.at[there, cols[k]], rep_slices.at[i - 1, :, cols[k]], pair(s_g2, k, i - 1), (column(i) * 2 + c, e))

    def g3_copy(k, i):
        return remote(rep_full.at[here, cols[k]], rep_full.at[here, cols[k]], pair(s_g3, k, i - 1), (column(i) * 2 + c, e))

    def g4_copy(k):
        return remote(rep_full.at[:, cols[k]], rep_full.at[:, cols[k]], pair(s_g4, k), sibling)

    def tiles(k, body):
        wide = 256 if WIDTHS[k] % 256 == 0 else 128

        def block(n, carry):
            body(pl.ds(pl.multiple_of(starts[k] + n * wide, 128), wide))
            return carry

        lax.fori_loop(0, WIDTHS[k] // wide, block, 0)

    def product(k):
        pltpu.make_async_copy(recv.at[:, :, cols[k]], recv.at[:, :, cols[k]], s_a.at[1, k]).wait()
        if k + AHEAD + 1 < count:
            rows_start(k + AHEAD + 1)

        def body(at):
            right = recv[:, :, at].reshape(ROWS, at.size)
            own = jnp.dot(left[0 : 2 * HID, :], right, preferred_element_type=F32)
            prod[0:HID, at] = own[0:HID]
            own_q[:, at], own_s[:, at] = coded(own[HID:])
            prod[HID:, at] = jnp.dot(left[2 * HID :, :], right, preferred_element_type=F32)

        tiles(k, body)
        sib_copy(k).start()
        each(own_copy(k), "start")
        if k == STATE_AT:
            each(loads[1:], "start")

            @pl.when(o == 1)
            def _():
                each(states, "start")

    def chip_sum(k):
        sib_copy(k).wait_recv()
        sib_in[:, cols[k]] += prod[hot_mine, cols[k]]

        @pl.when(o == 1)
        def _():
            def body(at):
                ring_q[:, at], ring_s[:, at] = coded(sib_in[:, at])

            tiles(k, body)
            each(ring_copy(k), "start")

    def scatter(k):
        @pl.when(o == 0)
        def _():
            each(ring_copy(k), "wait_recv")

            def body(at):
                for j in range(4):
                    rows = pl.ds(j * 32, 32)
                    part = sib_in[rows, at] + decoded(ring_qi[rows, at], ring_si[:, at])
                    sib_in[rows, at] = part
                    rs_q[rows, at], rs_s[j, :, at] = coded(part)

            tiles(k, body)
            for i in (2, 1, 3):
                each(rs_copy(k, i), "start")

    def gather(k):
        @pl.when(o == 0)
        def _():
            for i in (1, 3, 2):
                each(rs_copy(k, i), "wait_recv")

            def body(at):
                part = sib_in[here, at]
                for i in range(3):
                    part = part + decoded(rs_qi[i, :, at], rs_si[i, :, at])
                total_q[here, at], total_s[zh, :, at] = coded(part)

            tiles(k, body)
            for i in (2, 1, 3):
                each(ag_copy(k, i), "start")

    def ag_wait(k, i, buffer, sems):
        there = pl.ds(pl.multiple_of(lax.rem(zh + 4 - i, 4) * 32, 32), 32)
        remote(buffer.at[there, cols[k]], buffer.at[there, cols[k]], pair(sems, k, i - 1), sibling).wait_recv()

    def adamw(old, first_old, second_old, gradient):
        first = beta_one * first_old.astype(F32) + (1.0 - beta_one) * gradient
        second = beta_two * second_old.astype(F32) + (1.0 - beta_two) * gradient * gradient
        direction = first / (bias_one * (jnp.sqrt(second * (1.0 / bias_two)) + epsilon))
        updated = old * (1.0 - learn_rate * weight_decay) - learn_rate * direction
        return updated, first.astype(BF16), second.astype(BF16)

    def belongs(group, w):
        return jnp.full((16, w), owner[0], jnp.int32) == jnp.full((16, w), group, jnp.int32)

    def blocks(k, body):
        def block(n, carry):
            at = (pl.ds(pl.multiple_of(n * 16, 16), 16), cols[k])
            body(at, decoded(total_q[at], total_s[lax.div(n, 2), :, cols[k]]))
            return carry

        lax.fori_loop(0, 8, block, 0)

    def replicate(k):
        if k == 0:
            for load in loads[1:]:
                load.wait()

        @pl.when(o == 0)
        def _():
            if k == 0:
                each(states, "wait_recv")
            for i in (1, 3, 2):
                frm = lax.rem(zh + 4 - i, 4)
                block = total_q.at[rows_at(frm), cols[k]]
                steps = total_s.at[frm, :, cols[k]]
                remote(block, block, pair(s_ag, k, i - 1, 0), sibling).wait_recv()
                remote(steps, steps, pair(s_ag, k, i - 1, 1), sibling).wait_recv()
            each(fwd_copy(k), "start")

            def body(at, hot):
                mine, other = belongs(g, WIDTHS[k]), belongs(sibling[0], WIDTHS[k])
                updated, _, _ = adamw(
                    jnp.where(mine, mst[at], sib_mst[at]),
                    jnp.where(mine, m1[at].astype(F32), sib_m1[at].astype(F32)),
                    jnp.where(mine, m2[at].astype(F32), sib_m2[at].astype(F32)),
                    hot,
                )
                rep[at] = jnp.where(mine | other, updated, 0.0).astype(BF16)

            blocks(k, body)
            for i in (2, 1, 3):
                g2_copy(k, i).start()

    def update(k):
        @pl.when(o == 1)
        def _():
            each(fwd_copy(k), "wait_recv")

        each(own_copy(k), "wait_recv")

        def body(at, hot):
            own = prod[at] + decoded(own_qi[at], own_si[:, cols[k]])
            gradient = jnp.where(belongs(g, WIDTHS[k]), hot, own)
            mst[at], m1[at], m2[at] = adamw(mst[at], m1[at], m2[at], gradient)

        blocks(k, body)

    def regather(k):
        @pl.when(o == 0)
        def _():
            for i in (1, 3, 2):
                g2_copy(k, i).wait_recv()
            rep_full[here, cols[k]] = (rep[here, cols[k]] + rep_slices[0, :, cols[k]]) + (
                rep_slices[1, :, cols[k]] + rep_slices[2, :, cols[k]]
            )
            for i in (2, 1, 3):
                g3_copy(k, i).start()

    def share(k):
        @pl.when(o == 0)
        def _():
            for i in (1, 3, 2):
                ag_wait(k, i, rep_full, s_g3)
            g4_copy(k).start()

    def finish(k):
        @pl.when(o == 1)
        def _():
            g4_copy(k).wait_recv()


    stages = [product, chip_sum, scatter, gather, replicate, regather, share, update, finish]
    order = sorted(
        (SPACING * k + i, -k * NEWEST, i, k) for k in range(count) for i in range(len(stages))
    )
    for _, _, i, k in order:
        stages[i](k)

    send_x.wait_send()
    for k in range(count):
        half = recv.at[0:15, :, cols[k]]
        remote(half, half, pair(s_a, k), sibling).wait_send()
        each(own_copy(k), "wait_send")
        sib_copy(k).wait_send()

        @pl.when(o == 1)
        def _():
            if k == 0:
                each(states, "wait_send")
            each(ring_copy(k), "wait_send")

        @pl.when(o == 0)
        def _():
            for i in (1, 2, 3):
                each(rs_copy(k, i), "wait_send")
                each(ag_copy(k, i), "wait_send")
                g2_copy(k, i).wait_send()
                g3_copy(k, i).wait_send()
            each(fwd_copy(k), "wait_send")
            g4_copy(k).wait_send()


def local(dy_rows, hidden_rows, row_counts, hot_owner, master, moment1, moment2):
    count = len(WIDTHS)
    dma = pltpu.SemaphoreType.DMA
    in_hbm = pl.BlockSpec(memory_space=pltpu.HBM)
    scalars = pl.BlockSpec(memory_space=pltpu.SMEM)
    return pl.pallas_call(
        kernel,
        name="expert_grad",
        out_shape=(
            pltpu.VMEM((1, 1, HID, WIN), F32),
            pltpu.VMEM((1, 1, HID, WIN), BF16),
            pltpu.VMEM((1, 1, HID, WIN), BF16),
            pltpu.VMEM((1, 1, HID, WIN), BF16),
        ),
        in_specs=[in_hbm, in_hbm, scalars, scalars, in_hbm, in_hbm, in_hbm],
        out_specs=(pl.BlockSpec(memory_space=pltpu.VMEM),) * 4,
        scratch_shapes=[
            pltpu.VMEM((16, 48, WIN), BF16),
            pltpu.VMEM((ROWS, HID), BF16),
            pltpu.VMEM((ROWS, HID), F32),
            pltpu.VMEM((ROWS, 4 * HID), F32),
            pltpu.VMEM((4 * HID, ROWS), BF16),
            pltpu.VMEM((ROWS // 2, 2 * HID), BF16),
            pltpu.VMEM((ROWS // 2, 2 * HID), BF16),
            pltpu.VMEM((3 * HID, WIN), F32),
            pltpu.VMEM((HID, WIN), I16),
            pltpu.VMEM((1, WIN), F32),
            pltpu.VMEM((HID, WIN), I16),
            pltpu.VMEM((1, WIN), F32),
            pltpu.VMEM((HID, WIN), F32),
            pltpu.VMEM((HID, WIN), I16),
            pltpu.VMEM((1, WIN), F32),
            pltpu.VMEM((HID, WIN), I16),
            pltpu.VMEM((1, WIN), F32),
            pltpu.VMEM((HID, WIN), I16),
            pltpu.VMEM((4, 1, WIN), F32),
            pltpu.VMEM((3, 32, WIN), I16),
            pltpu.VMEM((3, 1, WIN), F32),
            pltpu.VMEM((HID, WIN), I16),
            pltpu.VMEM((4, 1, WIN), F32),
            pltpu.VMEM((HID, WIN), F32),
            pltpu.VMEM((HID, WIN), BF16),
            pltpu.VMEM((HID, WIN), BF16),
            pltpu.VMEM((HID, WIN), BF16),
            pltpu.VMEM((3, 32, WIN), BF16),
            dma((4,)),
            dma((2, 3)),
            dma((2,)),
            dma((2, count)),
            dma((2, count, 2)),
            dma((2, count)),
            dma((2, count, 2)),
            dma((2, count, 3, 2)),
            dma((2, count, 3, 2)),
            dma((2, count, 2)),
            dma((2, count, 3)),
            dma((2, count, 3)),
            dma((2, count)),
        ],
        compiler_params=pltpu.CompilerParams(
            collective_id=0, has_side_effects=True, vmem_limit_bytes=52 * 2**20
        ),
        cost_estimate=pl.CostEstimate(
            flops=2 * 4 * HID * ROWS * WIN, bytes_accessed=16 * 2**20, transcendentals=HID * WIN
        ),
    )(dy_rows, hidden_rows, jnp.swapaxes(row_counts, 2, 3), hot_owner, master, moment1, moment2)


def solution(mesh):
    rows = P("group", "expert", None, None)
    return jax.shard_map(
        local,
        mesh=mesh,
        in_specs=(rows, rows, rows, P("expert"), rows, rows, rows),
        out_specs=(rows,) * 4,
        check_vma=False,
    )
```
